32 devices in a mesh: ctx: 8 (over z, x), fsdp: 4 (over y, core).
Axes of the slice: x: 2, y: 2, z: 4, core: 2. Of those that a mesh axis runs over, the one named last changes fastest.
Arguments:
- tokens: bfloat16 [4, 1024, 1024], P('fsdp', 'ctx'), may hold values from -6 to 6
- segments: int32 [4, 1024], P('fsdp'), may hold values from 0 to 2, as said below
- w_query: bfloat16 [1024, 512], P(('ctx', 'fsdp')), may hold values from -0.1875 to 0.1875
- key_value_weight: bfloat16 [1024, 256], P(('ctx', 'fsdp')), may hold values from -0.1875 to 0.1875
- w_attn_out: bfloat16 [512, 1024], P(None, ('ctx', 'fsdp')), may hold values from -1 to 1
- w_zgate: bfloat16 [1024, 1536], P(('ctx', 'fsdp')), may hold values from -0.1875 to 0.1875
- w_conv_in: bfloat16 [1024, 1792], P(('ctx', 'fsdp')), may hold values from -0.1875 to 0.1875
- w_step: bfloat16 [1024, 24], P(('ctx', 'fsdp')), may hold values from -0.1875 to 0.1875
- w_mix_out: bfloat16 [1536, 1024], P(None, ('ctx', 'fsdp')), may hold values from -0.15625 to 0.15625
- w_gate_up: bfloat16 [1024, 4096], P(('ctx', 'fsdp')), may hold values from -0.1875 to 0.1875
- w_down: bfloat16 [2048, 1024], P(None, ('ctx', 'fsdp')), may hold values from -0.125 to 0.125
- gain_in: float32 [1024], replicated, may hold values from 0.5 to 1.5
- gain_ffn: float32 [1024], replicated, may hold values from 0.5 to 1.5
- gain_mix: float32 [1536], replicated, may hold values from 0.5 to 1.5
- conv_weight: float32 [4, 1792], replicated, may hold values from -3 to 3
- conv_bias: float32 [1792], replicated, may hold values from -0.5 to 0.5
- step_bias: float32 [24], replicated, may hold values from -6 to 0
- decay_log: float32 [24], replicated, may hold values from -4.5 to -1
- skip_gain: float32 [24], replicated, may hold values from 0.5 to 1.5
- cotangent: bfloat16 [4, 1024, 1024], P('fsdp', 'ctx'), may hold values from -6 to 6
Outputs:
- output: bfloat16 [4, 1024, 1024], P('fsdp', 'ctx')
- grad_tokens: float32 [4, 1024, 1024], P('fsdp', 'ctx')
- grad_query: float32 [1024, 512], P(('ctx', 'fsdp'))
- grad_keyval: float32 [1024, 256], P(('ctx', 'fsdp'))
- grad_attn_out: float32 [512, 1024], P(None, ('ctx', 'fsdp'))
- grad_zgate: float32 [1024, 1536], P(('ctx', 'fsdp'))
- grad_conv_in: float32 [1024, 1792], P(('ctx', 'fsdp'))
- grad_step: float32 [1024, 24], P(('ctx', 'fsdp'))
- grad_mix_out: float32 [1536, 1024], P(None, ('ctx', 'fsdp'))
- grad_gate_up: float32 [1024, 4096], P(('ctx', 'fsdp'))
- grad_down: float32 [2048, 1024], P(None, ('ctx', 'fsdp'))
- grad_gain_in: float32 [1024], replicated
- grad_gain_ffn: float32 [1024], replicated
- grad_gain_mix: float32 [1536], replicated
- grad_conv_weight: float32 [4, 1792], replicated
- grad_conv_bias: float32 [1792], replicated
- grad_step_bias: float32 [24], replicated
- grad_decay_log: float32 [24], replicated
- grad_skip_gain: float32 [24], replicated
The draws below stay inside these ranges and needn't reach their ends.
Inputs may be any that keep to these rules, and one draw needn't show every extreme that they name: `segments`: each row holds three documents numbered 0, 1, 2 in order: document 0 ends within the first 128 tokens of the row and document 2 begins within its last 128 tokens.
All inputs are finite; a program needn't handle non-finite values.
Results may differ from the reference program's by a relative error of at most 0.014.
Values may be sent and summed in bfloat16 or wider, within the bound.
A program may use at most 256 MiB of HBM per device.

```python
import jax
import jax.numpy as jnp
from jax import lax

MODEL_WIDTH = 1024
QUERY_HEADS = 8
KEY_VALUE_HEADS = 2
HEAD_SIZE = 64
MH = 24
MP = 64
NS = 128
FF = 2048
KC = 4
TOK_DEV = 128
DI = 1536
XBC = 1792
LENGTH = 1024
ROWS = 4
N_CTX = 8


def draw_segments(key, part):
    key = jax.random.fold_in(key, 11)
    first_key, last_key = jax.random.split(key)
    token_length = TOK_DEV * N_CTX
    first_end = jax.random.randint(first_key, (ROWS, 1), 1, TOK_DEV)
    last_start = jax.random.randint(last_key, (ROWS, 1), token_length - TOK_DEV + 1, token_length)
    places = jnp.arange(token_length, dtype=jnp.int32)[None, :]
    return (places >= first_end).astype(jnp.int32) + (places >= last_start).astype(jnp.int32)


def levels(stream_key, extent, shards, low, high):
    level = 1.0
    for position, parts in shards:
        steps = jax.random.uniform(jax.random.fold_in(jax.random.fold_in(stream_key, 6), position), (parts,), jnp.float32, low / len(shards), high / len(shards))
        level = level * jnp.repeat(jnp.exp(steps), extent[position] // parts).reshape((-1,) + (1,) * (len(extent) - 1 - position))
    return level


def centred(key, dims, scale, reach, pieces=(), held_as=jnp.bfloat16):
    drawn = scale * jax.random.normal(key, dims, jnp.float32)
    if pieces:
        drawn = drawn * levels(key, dims, pieces, -0.22, 0.18)
    return jnp.clip(drawn, -reach, reach).astype(held_as)


def setup_inputs(seed: int = 0) -> dict:
    splits = jax.random.split(jax.random.key(seed), 21)
    tokens = centred(splits[0], (ROWS, LENGTH, MODEL_WIDTH), 1.0, 6.0, ((0, 4), (1, 8)))
    segments = draw_segments(jax.random.fold_in(splits[20], 71), 0)
    w_query = centred(splits[2], (MODEL_WIDTH, QUERY_HEADS * HEAD_SIZE), MODEL_WIDTH ** -0.5, 0.1875, ((0, 32),))
    key_value_weight = centred(splits[3], (MODEL_WIDTH, 2 * KEY_VALUE_HEADS * HEAD_SIZE), MODEL_WIDTH ** -0.5, 0.1875, ((0, 32),))
    w_attn_out = centred(splits[4], (QUERY_HEADS * HEAD_SIZE, MODEL_WIDTH), (QUERY_HEADS * HEAD_SIZE // 16) ** -0.5, 1.0, ((1, 32),))
    w_zgate = centred(splits[5], (MODEL_WIDTH, DI), MODEL_WIDTH ** -0.5, 0.1875, ((0, 32),))
    w_conv_in = centred(splits[6], (MODEL_WIDTH, XBC), MODEL_WIDTH ** -0.5, 0.1875, ((0, 32),))
    w_step = centred(splits[7], (MODEL_WIDTH, MH), MODEL_WIDTH ** -0.5, 0.1875, ((0, 32),))
    w_mix_out = centred(splits[8], (DI, MODEL_WIDTH), DI ** -0.5, 0.15625, ((1, 32),))
    w_gate_up = centred(splits[9], (MODEL_WIDTH, 2 * FF), MODEL_WIDTH ** -0.5, 0.1875, ((0, 32),))
    w_down = centred(splits[10], (FF, MODEL_WIDTH), FF ** -0.5, 0.125, ((1, 32),))
    gain_in = jnp.clip(1.0 + 0.1 * jax.random.normal(splits[11], (MODEL_WIDTH,), jnp.float32), 0.5, 1.5)
    gain_ffn = jnp.clip(1.0 + 0.1 * jax.random.normal(splits[12], (MODEL_WIDTH,), jnp.float32), 0.5, 1.5)
    gain_mix = jnp.clip(1.0 + 0.1 * jax.random.normal(splits[13], (DI,), jnp.float32), 0.5, 1.5)
    conv_weight = centred(splits[14], (KC, XBC), 0.5, 3.0, (), jnp.float32)
    conv_bias = jnp.clip(jax.random.uniform(splits[15], (XBC,), jnp.float32, -0.5, 0.5), -0.5, 0.5)
    step_bias = jnp.clip(jax.random.uniform(splits[16], (MH,), jnp.float32, -6.0, 0.0), -6.0, 0.0)
    decay_log = jnp.clip(jax.random.uniform(splits[17], (MH,), jnp.float32, -4.5, -1.0), -4.5, -1.0)
    skip_gain = jnp.clip(jax.random.uniform(splits[18], (MH,), jnp.float32, 0.5, 1.5), 0.5, 1.5)
    cotangent = centred(splits[19], (ROWS, LENGTH, MODEL_WIDTH), 1.0, 6.0, ((0, 4), (1, 8)))
    return dict(tokens=tokens, segments=segments, w_query=w_query, key_value_weight=key_value_weight, w_attn_out=w_attn_out, w_zgate=w_zgate, w_conv_in=w_conv_in, w_step=w_step, w_mix_out=w_mix_out, w_gate_up=w_gate_up, w_down=w_down, gain_in=gain_in, gain_ffn=gain_ffn, gain_mix=gain_mix, conv_weight=conv_weight, conv_bias=conv_bias, step_bias=step_bias, decay_log=decay_log, skip_gain=skip_gain, cotangent=cotangent)


norm_eps = 1e-05
rope_base = 100000000000.0
highest = lax.Precision.HIGHEST
score_masked = -1e+30

@jax.custom_vjp
def lower_bound(v):
    return lax.optimization_barrier(v.astype(jnp.bfloat16)).astype(jnp.float32)

@jax.custom_vjp
def low_back(v):
    return v

def low_keep(v):
    return (lower_bound(v), None)

def low_pass(kept, grad):
    return (grad,)

def back_keep(v):
    return (v, None)

def back_low(kept, grad):
    return (lower_bound(grad),)
lower_bound.defvjp(low_keep, low_pass)
low_back.defvjp(back_keep, back_low)

def rms_scale(values, gain):
    return values * lax.rsqrt(lax.optimization_barrier(jnp.mean(values * values, axis=-1, keepdims=True)) + norm_eps) * gain

def apply_rotation(values, cosine_table, sine_table):
    half = values.shape[-1] // 2
    turned = jnp.concatenate([-values[..., half:], values[..., :half]], axis=-1)
    return values * cosine_table + turned * sine_table

def angles(positions, width):
    freq = rope_base ** (-jnp.arange(0, width, 2).astype(jnp.float32) / width)
    phase = positions.astype(jnp.float32)[:, None] * freq[None, :]
    phase = jnp.concatenate([phase, phase], axis=-1)
    return (jnp.cos(phase), jnp.sin(phase))

def attend_row(query_matrix, key_value_pair, seg_row):
    token_length = query_matrix.shape[0]
    block_length = min(512, token_length)
    group_width = QUERY_HEADS // KEY_VALUE_HEADS
    key_matrix = key_value_pair[:, :KEY_VALUE_HEADS * HEAD_SIZE].reshape(token_length, KEY_VALUE_HEADS, HEAD_SIZE)
    value_matrix = key_value_pair[:, KEY_VALUE_HEADS * HEAD_SIZE:].reshape(token_length, KEY_VALUE_HEADS, HEAD_SIZE)
    block_list = token_length // block_length
    positions = jnp.arange(token_length, dtype=jnp.int32)
    query_block_list = query_matrix.reshape(block_list, block_length, KEY_VALUE_HEADS, group_width, HEAD_SIZE)
    seg_blocks = seg_row.reshape(block_list, block_length)
    pos_blocks = positions.reshape(block_list, block_length)

    def one_block(inputs):
        query_block, seg_block, pos_block = inputs
        scores = jnp.einsum('qkgd,skd->kgqs', query_block, key_matrix, precision=highest) * HEAD_SIZE ** (-0.5)
        scores = low_back(scores)
        allowed = (positions[None, :] <= pos_block[:, None]) & (seg_row[None, :] == seg_block[:, None])
        scores = jnp.where(allowed[None, None], scores, score_masked)
        weights = lower_bound(jax.nn.softmax(scores, axis=-1))
        return jnp.einsum('kgqs,skd->qkgd', weights, value_matrix, precision=highest)
    result = lax.map(jax.checkpoint(one_block), (query_block_list, seg_blocks, pos_blocks))
    return result.reshape(token_length, QUERY_HEADS * HEAD_SIZE)

def span_terms(mix_input, b_proj, c_proj, step_size, rate, seg_span, seg_before):
    count_rows = mix_input.shape[0]
    log_decay = jnp.cumsum(rate, axis=0)
    places = jnp.arange(count_rows)
    allowed = (places[None, :] <= places[:, None]) & (seg_span[None, :] == seg_span[:, None])
    spread = jnp.exp(jnp.where(allowed[:, :, None], log_decay[:, None, :] - log_decay[None, :, :], -10000.0))
    inner = jnp.dot(c_proj, b_proj.T, precision=highest)
    mixing = spread * inner[:, :, None] * step_size[None, :, :]
    y_local = jnp.einsum('tsh,shp->thp', mixing, mix_input, precision=highest)
    coef_in = jnp.exp(log_decay) * (seg_span == seg_before)[:, None]
    last_segment = seg_span[-1]
    tail_weight = jnp.exp(log_decay[-1][None, :] - log_decay) * (seg_span == last_segment)[:, None] * step_size
    state_local = jnp.einsum('sh,shp,sn->hpn', tail_weight, mix_input, b_proj, precision=highest)
    end_decay = jnp.exp(log_decay[-1]) * (last_segment == seg_before)
    return (y_local, coef_in, end_decay, state_local)

def mamba_row(conv_low, gate_values, step_raw, seg_row, gain_mix, conv_weight, conv_bias, step_bias, decay_log, skip_gain):
    token_length = conv_low.shape[0]
    padded = jnp.concatenate([jnp.zeros((KC - 1, XBC), conv_low.dtype), conv_low], axis=0)
    seg_pad = jnp.concatenate([jnp.full((KC - 1,), -1, jnp.int32), seg_row])
    conv_sum = conv_bias + jnp.zeros_like(conv_low)
    for tap in range(KC):
        same = seg_pad[tap:tap + token_length] == seg_row
        conv_sum = conv_sum + conv_weight[tap] * jnp.where(same[:, None], padded[tap:tap + token_length], 0.0)
    activated = jax.nn.silu(conv_sum)
    mix_input = activated[:, :DI].reshape(token_length, MH, MP)
    b_proj = activated[:, DI:DI + NS]
    c_proj = activated[:, DI + NS:]
    step_size = jax.nn.softplus(step_raw + step_bias)
    rate = step_size * -jnp.exp(decay_log)
    spans = token_length // TOK_DEV
    lasts = seg_row[TOK_DEV - 1::TOK_DEV]
    befores = jnp.concatenate([jnp.full((1,), -1, jnp.int32), lasts[:-1]])
    inputs = (mix_input.reshape(spans, TOK_DEV, MH, MP), b_proj.reshape(spans, TOK_DEV, NS), c_proj.reshape(spans, TOK_DEV, NS), step_size.reshape(spans, TOK_DEV, MH), rate.reshape(spans, TOK_DEV, MH), seg_row.reshape(spans, TOK_DEV), befores)

    def span_step(state_in, span):
        x_span, b_span, c_span, step_span, rate_span, seg_span, seg_before = span
        y_local, coef_in, end_decay, state_local = span_terms(x_span, b_span, c_span, step_span, rate_span, seg_span, seg_before)
        carried = jnp.einsum('tn,hpn->thp', c_span, state_in, precision=highest)
        y_span = y_local + coef_in[:, :, None] * carried + skip_gain[None, :, None] * x_span
        state_out = end_decay[:, None, None] * state_in + state_local
        return (state_out, y_span)
    start_state = jnp.zeros((MH, MP, NS), conv_low.dtype)
    _, y_spans = lax.scan(jax.checkpoint(span_step), start_state, inputs)
    gated = y_spans.reshape(token_length, DI) * jax.nn.silu(gate_values)
    return rms_scale(gated, gain_mix)

def row_forward(params, row_x, seg_row):
    w_query, key_value_weight, w_attn_out, w_zgate, w_conv_in, w_step, w_mix_out, w_gate_up, w_down, gain_in, gain_ffn, gain_mix, conv_weight, conv_bias, step_bias, decay_log, skip_gain = params
    token_length = row_x.shape[0]
    normed = lower_bound(rms_scale(row_x, gain_in))
    cosine_table, sine_table = angles(jnp.arange(token_length, dtype=jnp.int32), HEAD_SIZE)
    query_matrix = low_back(jnp.dot(normed, w_query, precision=highest)).reshape(token_length, QUERY_HEADS, HEAD_SIZE)
    query_matrix = lower_bound(apply_rotation(query_matrix, cosine_table[:, None], sine_table[:, None]))
    key_value_pair = low_back(jnp.dot(normed, key_value_weight, precision=highest))
    key_matrix = apply_rotation(key_value_pair[:, :KEY_VALUE_HEADS * HEAD_SIZE].reshape(token_length, KEY_VALUE_HEADS, HEAD_SIZE), cosine_table[:, None], sine_table[:, None])
    key_value_pair = lower_bound(jnp.concatenate([key_matrix.reshape(token_length, KEY_VALUE_HEADS * HEAD_SIZE), key_value_pair[:, KEY_VALUE_HEADS * HEAD_SIZE:]], axis=1))
    attention_result = lower_bound(low_back(attend_row(query_matrix, key_value_pair, seg_row)))
    attn_out = low_back(jnp.dot(attention_result, w_attn_out, precision=highest))
    gate_values = low_back(jnp.dot(normed, w_zgate, precision=highest))
    conv_low = lower_bound(low_back(jnp.dot(normed, w_conv_in, precision=highest)))
    step_raw = low_back(jnp.dot(normed, w_step, precision=highest))
    mixed = lower_bound(mamba_row(conv_low, gate_values, step_raw, seg_row, gain_mix, conv_weight, conv_bias, step_bias, decay_log, skip_gain))
    mix_out = low_back(jnp.dot(mixed, w_mix_out, precision=highest))
    hidden = row_x + attn_out + mix_out
    hnorm = lower_bound(rms_scale(hidden, gain_ffn))
    gate_up = low_back(jnp.dot(hnorm, w_gate_up, precision=highest))
    activated = lower_bound(jax.nn.silu(gate_up[:, :FF]) * gate_up[:, FF:])
    ffn_out = low_back(jnp.dot(activated, w_down, precision=highest))
    return hidden + ffn_out

def reference(tokens, segments, w_query, key_value_weight, w_attn_out, w_zgate, w_conv_in, w_step, w_mix_out, w_gate_up, w_down, gain_in, gain_ffn, gain_mix, conv_weight, conv_bias, step_bias, decay_log, skip_gain, cotangent):
    params = tuple((item.astype(jnp.float32) for item in (w_query, key_value_weight, w_attn_out, w_zgate, w_conv_in, w_step, w_mix_out, w_gate_up, w_down, gain_in, gain_ffn, gain_mix, conv_weight, conv_bias, step_bias, decay_log, skip_gain)))

    def row_step(totals, inputs):
        row_x, seg_row, row_grad = inputs

        def forward(weights, values):
            return row_forward(weights, values, seg_row)
        result, pull = jax.vjp(forward, params, row_x.astype(jnp.float32))
        grads, grad_x = pull(row_grad.astype(jnp.float32))
        totals = jax.tree.map(jnp.add, totals, grads)
        return (totals, (result.astype(jnp.bfloat16), grad_x))
    zero_filled = jax.tree.map(jnp.zeros_like, params)
    totals, (output, grad_tokens) = lax.scan(row_step, zero_filled, (tokens, segments, cotangent))
    return (output, grad_tokens, totals[0], totals[1], totals[2], totals[3], totals[4], totals[5], totals[6], totals[7], totals[8], totals[9], totals[10], totals[11], totals[12], totals[13], totals[14], totals[15], totals[16])
```

```python
from functools import partial

import jax
import jax.numpy as jnp
from jax import lax
from jax.sharding import PartitionSpec as P

QUERY_HEADS = 8
KEY_VALUE_HEADS = 2
HEAD_SIZE = 64
MH = 24
MP = 64
NS = 128
FF = 2048
KC = 4
DI = 1536
XBC = 1792


norm_eps = 1e-05
rope_base = 100000000000.0
highest = lax.Precision.HIGHEST
score_masked = -1e30
key_block = 512


def from_behind(block, axis, distance):
    devices = range(lax.axis_size(axis))
    route = [(i - distance, i) for i in devices if i - distance in devices]
    return lax.ppermute(block, axis, route)


def entering(decay, state, axis, sign):
    count = lax.axis_size(axis)
    heads, rows, width = state.shape

    def hop(decay, state, distance):
        packed = jnp.concatenate(
            [
                state.reshape(heads * rows, width),
                jnp.broadcast_to(decay[:, None], (heads, width)),
            ]
        ).astype(jnp.bfloat16)
        packed = from_behind(packed, axis, sign * distance).astype(jnp.float32)
        return (packed[heads * rows :, 0], packed[: heads * rows].reshape(state.shape))

    decay, state = hop(decay, state, 1)
    distance = 1
    while distance < count - 1:
        before_decay, before_state = hop(decay, state, distance)
        state = decay[:, None, None] * before_state + state
        decay = before_decay * decay
        distance *= 2
    return state


def swap_with(block, axis, distance):
    route = [(i, i ^ distance) for i in range(lax.axis_size(axis))]
    return lax.ppermute(block, axis, route)


def gather_rows(block, axis):
    count, index = (lax.axis_size(axis), lax.axis_index(axis))
    rows, width = block.shape
    distance, level = (count // 2, 0)
    while distance:
        other = swap_with(block, axis, distance)
        upper = (index & distance) != 0
        block = jnp.stack(
            [jnp.where(upper, other, block), jnp.where(upper, block, other)], axis=level
        )
        distance, level = (distance // 2, level + 1)
    return block.reshape(count * rows, width)


def scatter_rows(values, axis):
    count, index = (lax.axis_size(axis), lax.axis_index(axis))
    rows, width = (values.shape[0] // count, values.shape[1])
    distance, left = (1, count // 2)
    while left:
        pairs = values.reshape(left, 2, rows, width)
        upper = (index & distance) != 0
        kept = jnp.where(upper, pairs[:, 1], pairs[:, 0])
        sent = jnp.where(upper, pairs[:, 0], pairs[:, 1]).astype(jnp.bfloat16)
        values = kept + swap_with(sent, axis, distance).astype(jnp.float32)
        distance, left = (distance * 2, left // 2)
    return values.reshape(rows, width)


def rms_scale(values, gain):
    return values * lax.rsqrt(jnp.mean(values * values, axis=-1, keepdims=True) + norm_eps) * gain


def apply_rotation(values, cosine_table, sine_table):
    half = values.shape[-1] // 2
    turned = jnp.concatenate([-values[..., half:], values[..., :half]], axis=-1)
    return values * cosine_table + turned * sine_table


def angles(positions, width):
    freq = rope_base ** (-jnp.arange(0, width, 2).astype(jnp.float32) / width)
    phase = positions.astype(jnp.float32)[:, None] * freq[None, :]
    phase = jnp.concatenate([phase, phase], axis=-1)
    return (jnp.cos(phase), jnp.sin(phase))


def product(left, right):
    return jnp.dot(left, right, preferred_element_type=jnp.float32)


def product_left(left, right):
    return lax.dot_general(
        left, right, (((0,), (0,)), ((), ())), preferred_element_type=jnp.float32
    )


def product_right(left, right):
    return lax.dot_general(
        left, right, (((1,), (1,)), ((), ())), preferred_element_type=jnp.float32
    )


def block_scores(query_group_list, all_kv, block_index, seg_row, seg_own, positions, block_length):
    block_key_value = lax.dynamic_slice_in_dim(all_kv, block_index * block_length, block_length, 0)
    key_matrix = block_key_value[:, : KEY_VALUE_HEADS * HEAD_SIZE].reshape(
        block_length, KEY_VALUE_HEADS, HEAD_SIZE
    )
    raw_scores = jnp.einsum(
        "qkgd,skd->kgqs", query_group_list, key_matrix, preferred_element_type=jnp.float32
    ) * HEAD_SIZE ** (-0.5)
    key_pos = block_index * block_length + jnp.arange(block_length, dtype=jnp.int32)
    key_seg = lax.dynamic_slice_in_dim(seg_row, block_index * block_length, block_length, 0)
    allowed = (key_pos[None, :] <= positions[:, None]) & (key_seg[None, :] == seg_own[:, None])
    return (jnp.where(allowed[None, None], raw_scores, score_masked), block_key_value)


def attend_forward(query_batch, all_kv, seg_row, seg_own, positions, leading_block, required_flag):
    count_rows = query_batch.shape[0]
    block_length = min(key_block, all_kv.shape[0])
    group_width = QUERY_HEADS // KEY_VALUE_HEADS
    query_group_list = query_batch.reshape(count_rows, KEY_VALUE_HEADS, group_width, HEAD_SIZE)

    def first_pass(block_index, carry):
        running_max, running_sum = carry
        scores, block_key_value = block_scores(
            query_group_list, all_kv, block_index, seg_row, seg_own, positions, block_length
        )
        new_max = jnp.maximum(running_max, jnp.max(scores, axis=-1))
        running_sum = running_sum * jnp.exp(running_max - new_max) + jnp.sum(
            jnp.exp(scores - new_max[..., None]), axis=-1
        )
        return (new_max, running_sum)

    start_state = (
        jnp.full((KEY_VALUE_HEADS, group_width, count_rows), score_masked, jnp.float32),
        jnp.zeros((KEY_VALUE_HEADS, group_width, count_rows), jnp.float32),
    )
    running_max, running_sum = lax.fori_loop(leading_block, required_flag, first_pass, start_state)
    log_total = running_max + jnp.log(running_sum)

    def backward_sweep(block_index, weighted):
        scores, block_key_value = block_scores(
            query_group_list, all_kv, block_index, seg_row, seg_own, positions, block_length
        )
        weights = jnp.exp(scores - log_total[..., None]).astype(jnp.bfloat16)
        value_matrix = block_key_value[:, KEY_VALUE_HEADS * HEAD_SIZE :].reshape(
            block_length, KEY_VALUE_HEADS, HEAD_SIZE
        )
        return weighted + jnp.einsum(
            "kgqs,skd->qkgd", weights, value_matrix, preferred_element_type=jnp.float32
        )

    weighted = lax.fori_loop(
        leading_block,
        required_flag,
        backward_sweep,
        jnp.zeros((count_rows, KEY_VALUE_HEADS, group_width, HEAD_SIZE), jnp.float32),
    )
    return (weighted.reshape(count_rows, QUERY_HEADS * HEAD_SIZE), log_total)


def attend_backward(
    query_batch,
    all_kv,
    gradient_batch,
    attention_result,
    log_total,
    seg_row,
    seg_own,
    positions,
    leading_block,
    required_flag,
):
    count_rows = query_batch.shape[0]
    group_width = QUERY_HEADS // KEY_VALUE_HEADS
    token_length = all_kv.shape[0]
    block_length = min(key_block, token_length)
    query_group_list = query_batch.reshape(count_rows, KEY_VALUE_HEADS, group_width, HEAD_SIZE)
    gradient_groups = gradient_batch.reshape(count_rows, KEY_VALUE_HEADS, group_width, HEAD_SIZE)
    row_dot = jnp.einsum(
        "qkgd,qkgd->kgq",
        gradient_groups.astype(jnp.float32),
        attention_result.reshape(count_rows, KEY_VALUE_HEADS, group_width, HEAD_SIZE),
    )

    def one_block(block_index, carry):
        grad_query, grad_kv = carry
        scores, block_key_value = block_scores(
            query_group_list, all_kv, block_index, seg_row, seg_own, positions, block_length
        )
        weights = jnp.exp(scores - log_total[..., None])
        key_matrix = block_key_value[:, : KEY_VALUE_HEADS * HEAD_SIZE].reshape(
            block_length, KEY_VALUE_HEADS, HEAD_SIZE
        )
        value_matrix = block_key_value[:, KEY_VALUE_HEADS * HEAD_SIZE :].reshape(
            block_length, KEY_VALUE_HEADS, HEAD_SIZE
        )
        grad_weights = jnp.einsum(
            "qkgd,skd->kgqs", gradient_groups, value_matrix, preferred_element_type=jnp.float32
        )
        grad_scores = (weights * (grad_weights - row_dot[..., None])).astype(jnp.bfloat16)
        grad_query = grad_query + jnp.einsum(
            "kgqs,skd->qkgd", grad_scores, key_matrix, preferred_element_type=jnp.float32
        ) * HEAD_SIZE ** (-0.5)
        gradient_key_rows = jnp.einsum(
            "kgqs,qkgd->skd", grad_scores, query_group_list, preferred_element_type=jnp.float32
        ) * HEAD_SIZE ** (-0.5)
        gradient_value_rows = jnp.einsum(
            "kgqs,qkgd->skd",
            weights.astype(jnp.bfloat16),
            gradient_groups,
            preferred_element_type=jnp.float32,
        )
        update = jnp.concatenate(
            [
                gradient_key_rows.reshape(block_length, KEY_VALUE_HEADS * HEAD_SIZE),
                gradient_value_rows.reshape(block_length, KEY_VALUE_HEADS * HEAD_SIZE),
            ],
            axis=1,
        )
        grad_kv = lax.dynamic_update_slice_in_dim(grad_kv, update, block_index * block_length, 0)
        return (grad_query, grad_kv)

    start_state = (
        jnp.zeros((count_rows, KEY_VALUE_HEADS, group_width, HEAD_SIZE), jnp.float32),
        jnp.zeros((token_length, 2 * KEY_VALUE_HEADS * HEAD_SIZE), jnp.float32),
    )
    grad_query, grad_kv = lax.fori_loop(leading_block, required_flag, one_block, start_state)
    return (grad_query.reshape(count_rows, QUERY_HEADS, HEAD_SIZE), grad_kv)


def conv_mix(extended, step_raw, conv_weight, conv_bias, step_bias, decay_log, seg_ext, seg_own):
    count_rows = step_raw.shape[0]
    conv_sum = conv_bias + jnp.zeros((count_rows, XBC), jnp.float32)
    for tap in range(KC):
        same = seg_ext[tap : tap + count_rows] == seg_own
        conv_sum = conv_sum + conv_weight[tap] * jnp.where(
            same[:, None], extended[tap : tap + count_rows], 0.0
        )
    activated = jax.nn.silu(conv_sum)
    step_size = jax.nn.softplus(step_raw + step_bias)
    log_decay = jnp.cumsum(step_size * -jnp.exp(decay_log), axis=0)
    return (activated, step_size, log_decay)


def split_inputs(activated):
    count_rows = activated.shape[0]
    return (
        activated[:, :DI].reshape(count_rows, MH, MP),
        activated[:, DI : DI + NS],
        activated[:, DI + NS :],
    )


def compute_end_state(activated, step_size, log_decay, seg_own, seg_before):
    mix_input, b_proj, c_proj = split_inputs(activated)
    last_segment = seg_own[-1]
    tail_weight = (
        jnp.exp(log_decay[-1][None, :] - log_decay) * (seg_own == last_segment)[:, None] * step_size
    )
    state_local = jnp.einsum("sh,shp,sn->hpn", tail_weight, mix_input, b_proj, precision=highest)
    end_decay = jnp.exp(log_decay[-1]) * (last_segment == seg_before)
    return (end_decay, state_local)


def mix_output(
    activated, step_size, log_decay, gate_values, skip_gain, gain_mix, state_in, seg_own, seg_before
):
    count_rows = activated.shape[0]
    mix_input, b_proj, c_proj = split_inputs(activated)
    places = jnp.arange(count_rows)
    allowed = (places[None, :] <= places[:, None]) & (seg_own[None, :] == seg_own[:, None])
    spread = jnp.exp(
        jnp.where(allowed[:, :, None], log_decay[:, None, :] - log_decay[None, :, :], -10000.0)
    )
    inner = jnp.dot(c_proj, b_proj.T, precision=highest)
    mixing = spread * inner[:, :, None] * step_size[None, :, :]
    y_local = jnp.einsum("tsh,shp->thp", mixing, mix_input, precision=highest)
    coef_in = jnp.exp(log_decay) * (seg_own == seg_before)[:, None]
    carried = jnp.einsum("tn,hpn->thp", c_proj, state_in, precision=highest)
    y_total = y_local + coef_in[:, :, None] * carried + skip_gain[None, :, None] * mix_input
    gated = y_total.reshape(count_rows, DI) * jax.nn.silu(gate_values)
    return rms_scale(gated, gain_mix)


def gate_product(gate_up):
    return jax.nn.silu(gate_up[:, :FF]) * gate_up[:, FF:]


def per_device(
    tokens,
    segments,
    w_query,
    key_value_weight,
    w_attn_out,
    w_zgate,
    w_conv_in,
    w_step,
    w_mix_out,
    w_gate_up,
    w_down,
    gain_in,
    gain_ffn,
    gain_mix,
    conv_weight,
    conv_bias,
    step_bias,
    decay_log,
    skip_gain,
    cotangent,
):
    count_rows = tokens.shape[1]
    block_length = min(key_block, count_rows * lax.axis_size("ctx"))
    row_start = lax.axis_index("ctx") * count_rows
    seg_row = segments[0]
    seg_own = lax.dynamic_slice_in_dim(seg_row, row_start, count_rows, 0)
    seg_pad = jnp.concatenate([jnp.full((KC - 1,), -1, jnp.int32), seg_row])
    seg_ext = lax.dynamic_slice_in_dim(seg_pad, row_start, count_rows + KC - 1, 0)
    seg_before = seg_ext[KC - 2]
    positions = row_start + jnp.arange(count_rows, dtype=jnp.int32)
    leading_block = jnp.sum((seg_row < seg_own[0]).astype(jnp.int32)) // block_length
    required_flag = positions[-1] // block_length + 1
    every = ("ctx", "fsdp")
    in_widths = [
        part.shape[1] for part in (w_query, key_value_weight, w_zgate, w_conv_in, w_step)
    ]
    in_cuts = [sum(in_widths[:k]) for k in range(1, 6)]
    padding = -in_cuts[-1] % 128
    w_in = lax.all_gather(
        jnp.pad(
            jnp.concatenate([w_query, key_value_weight, w_zgate, w_conv_in, w_step], axis=1),
            ((0, 0), (0, padding)),
        ),
        every,
        axis=0,
        tiled=True,
    )
    w_rest = lax.all_gather(
        jnp.concatenate([w_attn_out.T, w_mix_out.T, w_gate_up, w_down.T], axis=1),
        every,
        axis=0,
        tiled=True,
    )
    attn_width = QUERY_HEADS * HEAD_SIZE
    out_full = w_rest[:, : attn_width + DI]
    gate_up_full = w_rest[:, attn_width + DI : attn_width + DI + 2 * FF]
    down_full = w_rest[:, attn_width + DI + 2 * FF :]
    x_rows = tokens[0].astype(jnp.float32)
    normed, pull_in = jax.vjp(rms_scale, x_rows, gain_in)
    normed_b = normed.astype(jnp.bfloat16)
    from_normed = product(normed_b, w_in)
    query_raw, key_value_pair, gate_values, conv_raw, step_raw = jnp.split(
        from_normed[:, : in_cuts[-1]], in_cuts[:-1], axis=1
    )
    cosine_table, sine_table = angles(positions, HEAD_SIZE)
    query_rot = apply_rotation(
        query_raw.reshape(count_rows, QUERY_HEADS, HEAD_SIZE),
        cosine_table[:, None],
        sine_table[:, None],
    )
    query_batch = query_rot.astype(jnp.bfloat16)
    key_rotated = apply_rotation(
        key_value_pair[:, : KEY_VALUE_HEADS * HEAD_SIZE].reshape(
            count_rows, KEY_VALUE_HEADS, HEAD_SIZE
        ),
        cosine_table[:, None],
        sine_table[:, None],
    )
    keyval_b = jnp.concatenate(
        [
            key_rotated.reshape(count_rows, KEY_VALUE_HEADS * HEAD_SIZE),
            key_value_pair[:, KEY_VALUE_HEADS * HEAD_SIZE :],
        ],
        axis=1,
    ).astype(jnp.bfloat16)
    all_kv = gather_rows(keyval_b, "ctx")
    attention_result, log_total = attend_forward(
        query_batch, all_kv, seg_row, seg_own, positions, leading_block, required_flag
    )
    attended_b = attention_result.astype(jnp.bfloat16)
    conv_in_b = conv_raw.astype(jnp.bfloat16)
    before_rows = from_behind(conv_in_b[count_rows - (KC - 1) :], "ctx", 1)
    extended = jnp.concatenate([before_rows, conv_in_b], axis=0).astype(jnp.float32)
    (activated, step_size, log_decay), pull_pre = jax.vjp(
        partial(conv_mix, seg_ext=seg_ext, seg_own=seg_own),
        extended,
        step_raw,
        conv_weight,
        conv_bias,
        step_bias,
        decay_log,
    )
    (end_decay, state_local), pull_state = jax.vjp(
        partial(compute_end_state, seg_own=seg_own, seg_before=seg_before),
        activated,
        step_size,
        log_decay,
    )
    state_in = entering(end_decay, state_local, "ctx", 1)
    mixed, pull_mix = jax.vjp(
        partial(mix_output, seg_own=seg_own, seg_before=seg_before),
        activated,
        step_size,
        log_decay,
        gate_values,
        skip_gain,
        gain_mix,
        state_in,
    )
    mixed_b = mixed.astype(jnp.bfloat16)
    branches_b = jnp.concatenate([attended_b, mixed_b], axis=1)
    hidden = x_rows + product_right(branches_b, out_full)
    hnorm, pull_ffn = jax.vjp(rms_scale, hidden, gain_ffn)
    hnorm_b = hnorm.astype(jnp.bfloat16)
    gate_up = product(hnorm_b, gate_up_full)
    ffn_act, pull_act = jax.vjp(gate_product, gate_up)
    ffn_act_b = ffn_act.astype(jnp.bfloat16)
    result = hidden + product_right(ffn_act_b, down_full)
    grad_result = cotangent[0].astype(jnp.float32)
    grad_result_b = grad_result.astype(jnp.bfloat16)
    (grad_gate_up_rows,) = pull_act(product(grad_result_b, down_full))
    grad_gate_up_b = grad_gate_up_rows.astype(jnp.bfloat16)
    grad_hidden_norm, grad_gain_ffn = pull_ffn(product_right(grad_gate_up_b, gate_up_full))
    grad_hidden = grad_result + grad_hidden_norm
    grad_hidden_b = grad_hidden.astype(jnp.bfloat16)
    grad_rest = lax.psum_scatter(
        jnp.concatenate(
            [
                product_left(grad_hidden_b, branches_b).astype(jnp.bfloat16),
                product_left(hnorm_b, grad_gate_up_b).astype(jnp.bfloat16),
                product_left(grad_result_b, ffn_act_b).astype(jnp.bfloat16),
            ],
            axis=1,
        ),
        every,
        scatter_dimension=0,
        tiled=True,
    ).astype(jnp.float32)
    grad_attn_out = grad_rest[:, :attn_width].T
    grad_mix_out = grad_rest[:, attn_width : attn_width + DI].T
    grad_gate_up = grad_rest[:, attn_width + DI : attn_width + DI + 2 * FF]
    grad_down = grad_rest[:, attn_width + DI + 2 * FF :].T
    grad_branches = product(grad_hidden_b, out_full)
    grad_attended_b = grad_branches[:, :attn_width].astype(jnp.bfloat16)
    grad_mixed = grad_branches[:, attn_width:]
    grad_query_rot, grad_kv_all = attend_backward(
        query_batch,
        all_kv,
        grad_attended_b,
        attention_result,
        log_total,
        seg_row,
        seg_own,
        positions,
        leading_block,
        required_flag,
    )
    gradient_key_value_rows = scatter_rows(grad_kv_all, "ctx")
    grad_query_b = (
        apply_rotation(grad_query_rot, cosine_table[:, None], -sine_table[:, None])
        .reshape(count_rows, QUERY_HEADS * HEAD_SIZE)
        .astype(jnp.bfloat16)
    )
    gradient_key_prerotation = apply_rotation(
        gradient_key_value_rows[:, : KEY_VALUE_HEADS * HEAD_SIZE].reshape(
            count_rows, KEY_VALUE_HEADS, HEAD_SIZE
        ),
        cosine_table[:, None],
        -sine_table[:, None],
    )
    grad_keyval_b = jnp.concatenate(
        [
            gradient_key_prerotation.reshape(count_rows, KEY_VALUE_HEADS * HEAD_SIZE),
            gradient_key_value_rows[:, KEY_VALUE_HEADS * HEAD_SIZE :],
        ],
        axis=1,
    ).astype(jnp.bfloat16)
    (
        grad_act_mix,
        grad_step_mix,
        grad_decay_mix,
        grad_gate_values,
        grad_skip_gain,
        grad_gain_mix,
        grad_state_in,
    ) = pull_mix(grad_mixed)
    later_grads = entering(end_decay, grad_state_in, "ctx", -1)
    grad_end_decay = jnp.sum(later_grads * state_in, axis=(1, 2))
    grad_act_state, grad_step_state, grad_decay_state = pull_state((grad_end_decay, later_grads))
    (
        grad_extended,
        grad_step_raw,
        grad_conv_weight,
        grad_conv_bias,
        grad_step_bias,
        grad_decay_log,
    ) = pull_pre(
        (
            grad_act_mix + grad_act_state,
            grad_step_mix + grad_step_state,
            grad_decay_mix + grad_decay_state,
        )
    )
    from_next = from_behind(grad_extended[: KC - 1], "ctx", -1)
    grad_conv_rows = grad_extended[KC - 1 :].at[count_rows - (KC - 1) :].add(from_next)
    grad_conv_b = grad_conv_rows.astype(jnp.bfloat16)
    grad_gate_b = grad_gate_values.astype(jnp.bfloat16)
    grad_step_b = grad_step_raw.astype(jnp.bfloat16)
    grad_from_normed = jnp.pad(
        jnp.concatenate(
            [grad_query_b, grad_keyval_b, grad_gate_b, grad_conv_b, grad_step_b], axis=1
        ),
        ((0, 0), (0, padding)),
    )
    grad_in = lax.psum_scatter(
        product_left(normed_b, grad_from_normed).astype(jnp.bfloat16),
        every,
        scatter_dimension=0,
        tiled=True,
    ).astype(jnp.float32)
    grad_query, grad_keyval, grad_zgate, grad_conv_in, grad_step = jnp.split(
        grad_in[:, : in_cuts[-1]], in_cuts[:-1], axis=1
    )
    grad_normed = product_right(grad_from_normed, w_in)
    grad_x_norm, grad_gain_in = pull_in(grad_normed)
    grad_tokens = grad_hidden + grad_x_norm
    (
        sum_gain_in,
        sum_gain_ffn,
        sum_gain_mix,
        sum_conv_weight,
        sum_conv_bias,
        sum_step_bias,
        sum_decay_log,
        sum_skip_gain,
    ) = lax.psum(
        (
            grad_gain_in,
            grad_gain_ffn,
            grad_gain_mix,
            grad_conv_weight,
            grad_conv_bias,
            grad_step_bias,
            grad_decay_log,
            grad_skip_gain,
        ),
        ("ctx", "fsdp"),
    )
    return (
        result[None].astype(jnp.bfloat16),
        grad_tokens[None],
        grad_query,
        grad_keyval,
        grad_attn_out,
        grad_zgate,
        grad_conv_in,
        grad_step,
        grad_mix_out,
        grad_gate_up,
        grad_down,
        sum_gain_in,
        sum_gain_ffn,
        sum_gain_mix,
        sum_conv_weight,
        sum_conv_bias,
        sum_step_bias,
        sum_decay_log,
        sum_skip_gain,
    )


def solution(mesh):
    in_specs = (
        P("fsdp", "ctx", None),
        P("fsdp", None),
        P(("ctx", "fsdp"), None),
        P(("ctx", "fsdp"), None),
        P(None, ("ctx", "fsdp")),
        P(("ctx", "fsdp"), None),
        P(("ctx", "fsdp"), None),
        P(("ctx", "fsdp"), None),
        P(None, ("ctx", "fsdp")),
        P(("ctx", "fsdp"), None),
        P(None, ("ctx", "fsdp")),
        P(),
        P(),
        P(),
        P(),
        P(),
        P(),
        P(),
        P(),
        P("fsdp", "ctx", None),
    )
    out_specs = (
        P("fsdp", "ctx", None),
        P("fsdp", "ctx", None),
        P(("ctx", "fsdp"), None),
        P(("ctx", "fsdp"), None),
        P(None, ("ctx", "fsdp")),
        P(("ctx", "fsdp"), None),
        P(("ctx", "fsdp"), None),
        P(("ctx", "fsdp"), None),
        P(None, ("ctx", "fsdp")),
        P(("ctx", "fsdp"), None),
        P(None, ("ctx", "fsdp")),
        P(),
        P(),
        P(),
        P(),
        P(),
        P(),
        P(),
        P(),
    )
    return jax.shard_map(
        per_device, mesh=mesh, in_specs=in_specs, out_specs=out_specs, check_vma=False
    )
```

```python
from functools import partial

import jax
import jax.numpy as jnp
from jax import lax
from jax.sharding import PartitionSpec as P

QUERY_HEADS = 8
KEY_VALUE_HEADS = 2
HEAD_SIZE = 64
MH = 24
MP = 64
NS = 128
FF = 2048
KC = 4
DI = 1536
XBC = 1792


norm_eps = 1e-05
rope_base = 100000000000.0
highest = lax.Precision.HIGHEST
score_masked = -1e30
key_block = 512


def from_behind(block, axis, distance):
    devices = range(lax.axis_size(axis))
    route = [(i - distance, i) for i in devices if i - distance in devices]
    return lax.ppermute(block, axis, route)


def entering(decay, state, axis, sign):
    count = lax.axis_size(axis)
    heads, rows, width = state.shape

    def hop(decay, state, distance):
        packed = jnp.concatenate(
            [
                state.reshape(heads * rows, width),
                jnp.broadcast_to(decay[:, None], (heads, width)),
            ]
        ).astype(jnp.bfloat16)
        packed = from_behind(packed, axis, sign * distance).astype(jnp.float32)
        return (packed[heads * rows :, 0], packed[: heads * rows].reshape(state.shape))

    decay, state = hop(decay, state, 1)
    distance = 1
    while distance < count - 1:
        before_decay, before_state = hop(decay, state, distance)
        state = decay[:, None, None] * before_state + state
        decay = before_decay * decay
        distance *= 2
    return state


def swap_with(block, axis, distance):
    route = [(i, i ^ distance) for i in range(lax.axis_size(axis))]
    return lax.ppermute(block, axis, route)


def gather_rows(block, axis):
    count, index = (lax.axis_size(axis), lax.axis_index(axis))
    rows, width = block.shape
    distance, level = (count // 2, 0)
    while distance:
        other = swap_with(block, axis, distance)
        upper = (index & distance) != 0
        block = jnp.stack(
            [jnp.where(upper, other, block), jnp.where(upper, block, other)], axis=level
        )
        distance, level = (distance // 2, level + 1)
    return block.reshape(count * rows, width)


def scatter_rows(values, axis):
    count, index = (lax.axis_size(axis), lax.axis_index(axis))
    rows, width = (values.shape[0] // count, values.shape[1])
    distance, left = (1, count // 2)
    while left:
        pairs = values.reshape(left, 2, rows, width)
        upper = (index & distance) != 0
        kept = jnp.where(upper, pairs[:, 1], pairs[:, 0])
        sent = jnp.where(upper, pairs[:, 0], pairs[:, 1]).astype(jnp.bfloat16)
        values = kept + swap_with(sent, axis, distance).astype(jnp.float32)
        distance, left = (distance * 2, left // 2)
    return values.reshape(rows, width)


def rms_scale(values, gain):
    return values * lax.rsqrt(jnp.mean(values * values, axis=-1, keepdims=True) + norm_eps) * gain


def apply_rotation(values, cosine_table, sine_table):
    half = values.shape[-1] // 2
    turned = jnp.concatenate([-values[..., half:], values[..., :half]], axis=-1)
    return values * cosine_table + turned * sine_table


def angles(positions, width):
    freq = rope_base ** (-jnp.arange(0, width, 2).astype(jnp.float32) / width)
    phase = positions.astype(jnp.float32)[:, None] * freq[None, :]
    phase = jnp.concatenate([phase, phase], axis=-1)
    return (jnp.cos(phase), jnp.sin(phase))


def product(left, right):
    return jnp.dot(left, right, preferred_element_type=jnp.float32)


def product_left(left, right):
    return lax.dot_general(
        left, right, (((0,), (0,)), ((), ())), preferred_element_type=jnp.float32
    )


def product_right(left, right):
    return lax.dot_general(
        left, right, (((1,), (1,)), ((), ())), preferred_element_type=jnp.float32
    )


def block_scores(query_group_list, all_kv, block_index, seg_row, seg_own, positions, block_length):
    block_key_value = lax.dynamic_slice_in_dim(all_kv, block_index * block_length, block_length, 0)
    key_matrix = block_key_value[:, : KEY_VALUE_HEADS * HEAD_SIZE].reshape(
        block_length, KEY_VALUE_HEADS, HEAD_SIZE
    )
    raw_scores = jnp.einsum(
        "qkgd,skd->kgqs", query_group_list, key_matrix, preferred_element_type=jnp.float32
    ) * HEAD_SIZE ** (-0.5)
    key_pos = block_index * block_length + jnp.arange(block_length, dtype=jnp.int32)
    key_seg = lax.dynamic_slice_in_dim(seg_row, block_index * block_length, block_length, 0)
    allowed = (key_pos[None, :] <= positions[:, None]) & (key_seg[None, :] == seg_own[:, None])
    return (jnp.where(allowed[None, None], raw_scores, score_masked), block_key_value)


def attend_forward(query_batch, all_kv, seg_row, seg_own, positions, leading_block, required_flag):
    count_rows = query_batch.shape[0]
    block_length = min(key_block, all_kv.shape[0])
    group_width = QUERY_HEADS // KEY_VALUE_HEADS
    query_group_list = query_batch.reshape(count_rows, KEY_VALUE_HEADS, group_width, HEAD_SIZE)

    def first_pass(block_index, carry):
        running_max, running_sum = carry
        scores, block_key_value = block_scores(
            query_group_list, all_kv, block_index, seg_row, seg_own, positions, block_length
        )
        new_max = jnp.maximum(running_max, jnp.max(scores, axis=-1))
        running_sum = running_sum * jnp.exp(running_max - new_max) + jnp.sum(
            jnp.exp(scores - new_max[..., None]), axis=-1
        )
        return (new_max, running_sum)

    start_state = (
        jnp.full((KEY_VALUE_HEADS, group_width, count_rows), score_masked, jnp.float32),
        jnp.zeros((KEY_VALUE_HEADS, group_width, count_rows), jnp.float32),
    )
    running_max, running_sum = lax.fori_loop(leading_block, required_flag, first_pass, start_state)
    log_total = running_max + jnp.log(running_sum)

    def backward_sweep(block_index, weighted):
        scores, block_key_value = block_scores(
            query_group_list, all_kv, block_index, seg_row, seg_own, positions, block_length
        )
        weights = jnp.exp(scores - log_total[..., None]).astype(jnp.bfloat16)
        value_matrix = block_key_value[:, KEY_VALUE_HEADS * HEAD_SIZE :].reshape(
            block_length, KEY_VALUE_HEADS, HEAD_SIZE
        )
        return weighted + jnp.einsum(
            "kgqs,skd->qkgd", weights, value_matrix, preferred_element_type=jnp.float32
        )

    weighted = lax.fori_loop(
        leading_block,
        required_flag,
        backward_sweep,
        jnp.zeros((count_rows, KEY_VALUE_HEADS, group_width, HEAD_SIZE), jnp.float32),
    )
    return (weighted.reshape(count_rows, QUERY_HEADS * HEAD_SIZE), log_total)


def attend_backward(
    query_batch,
    all_kv,
    gradient_batch,
    attention_result,
    log_total,
    seg_row,
    seg_own,
    positions,
    leading_block,
    required_flag,
):
    count_rows = query_batch.shape[0]
    group_width = QUERY_HEADS // KEY_VALUE_HEADS
    token_length = all_kv.shape[0]
    block_length = min(key_block, token_length)
    query_group_list = query_batch.reshape(count_rows, KEY_VALUE_HEADS, group_width, HEAD_SIZE)
    gradient_groups = gradient_batch.reshape(count_rows, KEY_VALUE_HEADS, group_width, HEAD_SIZE)
    row_dot = jnp.einsum(
        "qkgd,qkgd->kgq",
        gradient_groups.astype(jnp.float32),
        attention_result.reshape(count_rows, KEY_VALUE_HEADS, group_width, HEAD_SIZE),
    )

    def one_block(block_index, carry):
        grad_query, grad_kv = carry
        scores, block_key_value = block_scores(
            query_group_list, all_kv, block_index, seg_row, seg_own, positions, block_length
        )
        weights = jnp.exp(scores - log_total[..., None])
        key_matrix = block_key_value[:, : KEY_VALUE_HEADS * HEAD_SIZE].reshape(
            block_length, KEY_VALUE_HEADS, HEAD_SIZE
        )
        value_matrix = block_key_value[:, KEY_VALUE_HEADS * HEAD_SIZE :].reshape(
            block_length, KEY_VALUE_HEADS, HEAD_SIZE
        )
        grad_weights = jnp.einsum(
            "qkgd,skd->kgqs", gradient_groups, value_matrix, preferred_element_type=jnp.float32
        )
        grad_scores = (weights * (grad_weights - row_dot[..., None])).astype(jnp.bfloat16)
        grad_query = grad_query + jnp.einsum(
            "kgqs,skd->qkgd", grad_scores, key_matrix, preferred_element_type=jnp.float32
        ) * HEAD_SIZE ** (-0.5)
        gradient_key_rows = jnp.einsum(
            "kgqs,qkgd->skd", grad_scores, query_group_list, preferred_element_type=jnp.float32
        ) * HEAD_SIZE ** (-0.5)
        gradient_value_rows = jnp.einsum(
            "kgqs,qkgd->skd",
            weights.astype(jnp.bfloat16),
            gradient_groups,
            preferred_element_type=jnp.float32,
        )
        update = jnp.concatenate(
            [
                gradient_key_rows.reshape(block_length, KEY_VALUE_HEADS * HEAD_SIZE),
                gradient_value_rows.reshape(block_length, KEY_VALUE_HEADS * HEAD_SIZE),
            ],
            axis=1,
        )
        grad_kv = lax.dynamic_update_slice_in_dim(grad_kv, update, block_index * block_length, 0)
        return (grad_query, grad_kv)

    start_state = (
        jnp.zeros((count_rows, KEY_VALUE_HEADS, group_width, HEAD_SIZE), jnp.float32),
        jnp.zeros((token_length, 2 * KEY_VALUE_HEADS * HEAD_SIZE), jnp.float32),
    )
    grad_query, grad_kv = lax.fori_loop(leading_block, required_flag, one_block, start_state)
    return (grad_query.reshape(count_rows, QUERY_HEADS, HEAD_SIZE), grad_kv)


def conv_mix(extended, step_raw, conv_weight, conv_bias, step_bias, decay_log, seg_ext, seg_own):
    count_rows = step_raw.shape[0]
    conv_sum = conv_bias + jnp.zeros((count_rows, XBC), jnp.float32)
    for tap in range(KC):
        same = seg_ext[tap : tap + count_rows] == seg_own
        conv_sum = conv_sum + conv_weight[tap] * jnp.where(
            same[:, None], extended[tap : tap + count_rows], 0.0
        )
    activated = jax.nn.silu(conv_sum)
    step_size = jax.nn.softplus(step_raw + step_bias)
    log_decay = jnp.cumsum(step_size * -jnp.exp(decay_log), axis=0)
    return (activated, step_size, log_decay)


def split_inputs(activated):
    count_rows = activated.shape[0]
    return (
        activated[:, :DI].reshape(count_rows, MH, MP),
        activated[:, DI : DI + NS],
        activated[:, DI + NS :],
    )


def compute_end_state(activated, step_size, log_decay, seg_own, seg_before):
    mix_input, b_proj, c_proj = split_inputs(activated)
    last_segment = seg_own[-1]
    tail_weight = (
        jnp.exp(log_decay[-1][None, :] - log_decay) * (seg_own == last_segment)[:, None] * step_size
    )
    state_local = jnp.einsum("sh,shp,sn->hpn", tail_weight, mix_input, b_proj, precision=highest)
    end_decay = jnp.exp(log_decay[-1]) * (last_segment == seg_before)
    return (end_decay, state_local)


def mix_output(
    activated, step_size, log_decay, gate_values, skip_gain, gain_mix, state_in, seg_own, seg_before
):
    count_rows = activated.shape[0]
    mix_input, b_proj, c_proj = split_inputs(activated)
    places = jnp.arange(count_rows)
    allowed = (places[None, :] <= places[:, None]) & (seg_own[None, :] == seg_own[:, None])
    spread = jnp.exp(
        jnp.where(allowed[:, :, None], log_decay[:, None, :] - log_decay[None, :, :], -10000.0)
    )
    inner = jnp.dot(c_proj, b_proj.T, precision=highest)
    mixing = spread * inner[:, :, None] * step_size[None, :, :]
    y_local = jnp.einsum("tsh,shp->thp", mixing, mix_input, precision=highest)
    coef_in = jnp.exp(log_decay) * (seg_own == seg_before)[:, None]
    carried = jnp.einsum("tn,hpn->thp", c_proj, state_in, precision=highest)
    y_total = y_local + coef_in[:, :, None] * carried + skip_gain[None, :, None] * mix_input
    gated = y_total.reshape(count_rows, DI) * jax.nn.silu(gate_values)
    return rms_scale(gated, gain_mix)


def gate_product(gate_up):
    return jax.nn.silu(gate_up[:, :FF]) * gate_up[:, FF:]


def per_device(
    tokens,
    segments,
    w_query,
    key_value_weight,
    w_attn_out,
    w_zgate,
    w_conv_in,
    w_step,
    w_mix_out,
    w_gate_up,
    w_down,
    gain_in,
    gain_ffn,
    gain_mix,
    conv_weight,
    conv_bias,
    step_bias,
    decay_log,
    skip_gain,
    cotangent,
):
    count_rows = tokens.shape[1]
    block_length = min(key_block, count_rows * lax.axis_size("ctx"))
    row_start = lax.axis_index("ctx") * count_rows
    seg_row = segments[0]
    seg_own = lax.dynamic_slice_in_dim(seg_row, row_start, count_rows, 0)
    seg_pad = jnp.concatenate([jnp.full((KC - 1,), -1, jnp.int32), seg_row])
    seg_ext = lax.dynamic_slice_in_dim(seg_pad, row_start, count_rows + KC - 1, 0)
    seg_before = seg_ext[KC - 2]
    positions = row_start + jnp.arange(count_rows, dtype=jnp.int32)
    leading_block = jnp.sum((seg_row < seg_own[0]).astype(jnp.int32)) // block_length
    required_flag = positions[-1] // block_length + 1
    every = ("ctx", "fsdp")
    in_widths = [
        part.shape[1] for part in (w_query, key_value_weight, w_zgate, w_conv_in, w_step)
    ]
    in_cuts = [sum(in_widths[:k]) for k in range(1, 6)]
    padding = -in_cuts[-1] % 128
    w_in = lax.all_gather(
        jnp.pad(
            jnp.concatenate([w_query, key_value_weight, w_zgate, w_conv_in, w_step], axis=1),
            ((0, 0), (0, padding)),
        ),
        every,
        axis=0,
        tiled=True,
    )
    w_rest = lax.all_gather(
        jnp.concatenate([w_attn_out.T, w_mix_out.T, w_gate_up, w_down.T], axis=1),
        every,
        axis=0,
        tiled=True,
    )
    attn_width = QUERY_HEADS * HEAD_SIZE
    out_full = w_rest[:, : attn_width + DI]
    gate_up_full = w_rest[:, attn_width + DI : attn_width + DI + 2 * FF]
    down_full = w_rest[:, attn_width + DI + 2 * FF :]
    x_rows = tokens[0].astype(jnp.float32)
    normed, pull_in = jax.vjp(rms_scale, x_rows, gain_in)
    normed_b = normed.astype(jnp.bfloat16)
    from_normed = product(normed_b, w_in)
    query_raw, key_value_pair, gate_values, conv_raw, step_raw = jnp.split(
        from_normed[:, : in_cuts[-1]], in_cuts[:-1], axis=1
    )
    cosine_table, sine_table = angles(positions, HEAD_SIZE)
    query_rot = apply_rotation(
        query_raw.reshape(count_rows, QUERY_HEADS, HEAD_SIZE),
        cosine_table[:, None],
        sine_table[:, None],
    )
    query_batch = query_rot.astype(jnp.bfloat16)
    key_rotated = apply_rotation(
        key_value_pair[:, : KEY_VALUE_HEADS * HEAD_SIZE].reshape(
            count_rows, KEY_VALUE_HEADS, HEAD_SIZE
        ),
        cosine_table[:, None],
        sine_table[:, None],
    )
    keyval_b = jnp.concatenate(
        [
            key_rotated.reshape(count_rows, KEY_VALUE_HEADS * HEAD_SIZE),
            key_value_pair[:, KEY_VALUE_HEADS * HEAD_SIZE :],
        ],
        axis=1,
    ).astype(jnp.bfloat16)
    all_kv = gather_rows(keyval_b, "ctx")
    attention_result, log_total = attend_forward(
        query_batch, all_kv, seg_row, seg_own, positions, leading_block, required_flag
    )
    attended_b = attention_result.astype(jnp.bfloat16)
    conv_in_b = conv_raw.astype(jnp.bfloat16)
    before_rows = from_behind(conv_in_b[count_rows - (KC - 1) :], "ctx", 1)
    extended = jnp.concatenate([before_rows, conv_in_b], axis=0).astype(jnp.float32)
    (activated, step_size, log_decay), pull_pre = jax.vjp(
        partial(conv_mix, seg_ext=seg_ext, seg_own=seg_own),
        extended,
        step_raw,
        conv_weight,
        conv_bias,
        step_bias,
        decay_log,
    )
    (end_decay, state_local), pull_state = jax.vjp(
        partial(compute_end_state, seg_own=seg_own, seg_before=seg_before),
        activated,
        step_size,
        log_decay,
    )
    state_in = entering(end_decay, state_local, "ctx", 1)
    mixed, pull_mix = jax.vjp(
        partial(mix_output, seg_own=seg_own, seg_before=seg_before),
        activated,
        step_size,
        log_decay,
        gate_values,
        skip_gain,
        gain_mix,
        state_in,
    )
    mixed_b = mixed.astype(jnp.bfloat16)
    branches_b = jnp.concatenate([attended_b, mixed_b], axis=1)
    hidden = x_rows + product_right(branches_b, out_full)
    hnorm, pull_ffn = jax.vjp(rms_scale, hidden, gain_ffn)
    hnorm_b = hnorm.astype(jnp.bfloat16)
    gate_up = product(hnorm_b, gate_up_full)
    ffn_act, pull_act = jax.vjp(gate_product, gate_up)
    ffn_act_b = ffn_act.astype(jnp.bfloat16)
    result = hidden + product_right(ffn_act_b, down_full)
    grad_result = cotangent[0].astype(jnp.float32)
    grad_result_b = grad_result.astype(jnp.bfloat16)
    (grad_gate_up_rows,) = pull_act(product(grad_result_b, down_full))
    grad_gate_up_b = grad_gate_up_rows.astype(jnp.bfloat16)
    grad_hidden_norm, grad_gain_ffn = pull_ffn(product_right(grad_gate_up_b, gate_up_full))
    grad_hidden = grad_result + grad_hidden_norm
    grad_hidden_b = grad_hidden.astype(jnp.bfloat16)
    grad_rest = lax.psum_scatter(
        jnp.concatenate(
            [
                product_left(grad_hidden_b, branches_b).astype(jnp.bfloat16),
                product_left(hnorm_b, grad_gate_up_b).astype(jnp.bfloat16),
                product_left(grad_result_b, ffn_act_b).astype(jnp.bfloat16),
            ],
            axis=1,
        ),
        every,
        scatter_dimension=0,
        tiled=True,
    ).astype(jnp.float32)
    grad_attn_out = grad_rest[:, :attn_width].T
    grad_mix_out = grad_rest[:, attn_width : attn_width + DI].T
    grad_gate_up = grad_rest[:, attn_width + DI : attn_width + DI + 2 * FF]
    grad_down = grad_rest[:, attn_width + DI + 2 * FF :].T
    grad_branches = product(grad_hidden_b, out_full)
    grad_attended_b = grad_branches[:, :attn_width].astype(jnp.bfloat16)
    grad_mixed = grad_branches[:, attn_width:]
    grad_query_rot, grad_kv_all = attend_backward(
        query_batch,
        all_kv,
        grad_attended_b,
        attention_result,
        log_total,
        seg_row,
        seg_own,
        positions,
        leading_block,
        required_flag,
    )
    gradient_key_value_rows = scatter_rows(grad_kv_all, "ctx")
    grad_query_b = (
        apply_rotation(grad_query_rot, cosine_table[:, None], -sine_table[:, None])
        .reshape(count_rows, QUERY_HEADS * HEAD_SIZE)
        .astype(jnp.bfloat16)
    )
    gradient_key_prerotation = apply_rotation(
        gradient_key_value_rows[:, : KEY_VALUE_HEADS * HEAD_SIZE].reshape(
            count_rows, KEY_VALUE_HEADS, HEAD_SIZE
        ),
        cosine_table[:, None],
        -sine_table[:, None],
    )
    grad_keyval_b = jnp.concatenate(
        [
            gradient_key_prerotation.reshape(count_rows, KEY_VALUE_HEADS * HEAD_SIZE),
            gradient_key_value_rows[:, KEY_VALUE_HEADS * HEAD_SIZE :],
        ],
        axis=1,
    ).astype(jnp.bfloat16)
    (
        grad_act_mix,
        grad_step_mix,
        grad_decay_mix,
        grad_gate_values,
        grad_skip_gain,
        grad_gain_mix,
        grad_state_in,
    ) = pull_mix(grad_mixed)
    later_grads = entering(end_decay, grad_state_in, "ctx", -1)
    grad_end_decay = jnp.sum(later_grads * state_in, axis=(1, 2))
    grad_act_state, grad_step_state, grad_decay_state = pull_state((grad_end_decay, later_grads))
    (
        grad_extended,
        grad_step_raw,
        grad_conv_weight,
        grad_conv_bias,
        grad_step_bias,
        grad_decay_log,
    ) = pull_pre(
        (
            grad_act_mix + grad_act_state,
            grad_step_mix + grad_step_state,
            grad_decay_mix + grad_decay_state,
        )
    )
    from_next = from_behind(grad_extended[: KC - 1], "ctx", -1)
    grad_conv_rows = grad_extended[KC - 1 :].at[count_rows - (KC - 1) :].add(from_next)
    grad_conv_b = grad_conv_rows.astype(jnp.bfloat16)
    grad_gate_b = grad_gate_values.astype(jnp.bfloat16)
    grad_step_b = grad_step_raw.astype(jnp.bfloat16)
    grad_from_normed = jnp.pad(
        jnp.concatenate(
            [grad_query_b, grad_keyval_b, grad_gate_b, grad_conv_b, grad_step_b], axis=1
        ),
        ((0, 0), (0, padding)),
    )
    after_rest = jnp.minimum(jnp.abs(grad_rest[0, 0]), 0.0)
    grad_in = lax.psum_scatter(
        (product_left(normed_b, grad_from_normed) + after_rest).astype(jnp.bfloat16),
        every,
        scatter_dimension=0,
        tiled=True,
    ).astype(jnp.float32)
    grad_query, grad_keyval, grad_zgate, grad_conv_in, grad_step = jnp.split(
        grad_in[:, : in_cuts[-1]], in_cuts[:-1], axis=1
    )
    grad_normed = product_right(grad_from_normed, w_in)
    grad_x_norm, grad_gain_in = pull_in(grad_normed)
    grad_tokens = grad_hidden + grad_x_norm
    (
        sum_gain_in,
        sum_gain_ffn,
        sum_gain_mix,
        sum_conv_weight,
        sum_conv_bias,
        sum_step_bias,
        sum_decay_log,
        sum_skip_gain,
    ) = lax.psum(
        (
            grad_gain_in,
            grad_gain_ffn,
            grad_gain_mix,
            grad_conv_weight,
            grad_conv_bias,
            grad_step_bias,
            grad_decay_log,
            grad_skip_gain,
        ),
        ("ctx", "fsdp"),
    )
    return (
        result[None].astype(jnp.bfloat16),
        grad_tokens[None],
        grad_query,
        grad_keyval,
        grad_attn_out,
        grad_zgate,
        grad_conv_in,
        grad_step,
        grad_mix_out,
        grad_gate_up,
        grad_down,
        sum_gain_in,
        sum_gain_ffn,
        sum_gain_mix,
        sum_conv_weight,
        sum_conv_bias,
        sum_step_bias,
        sum_decay_log,
        sum_skip_gain,
    )


def solution(mesh):
    in_specs = (
        P("fsdp", "ctx", None),
        P("fsdp", None),
        P(("ctx", "fsdp"), None),
        P(("ctx", "fsdp"), None),
        P(None, ("ctx", "fsdp")),
        P(("ctx", "fsdp"), None),
        P(("ctx", "fsdp"), None),
        P(("ctx", "fsdp"), None),
        P(None, ("ctx", "fsdp")),
        P(("ctx", "fsdp"), None),
        P(None, ("ctx", "fsdp")),
        P(),
        P(),
        P(),
        P(),
        P(),
        P(),
        P(),
        P(),
        P("fsdp", "ctx", None),
    )
    out_specs = (
        P("fsdp", "ctx", None),
        P("fsdp", "ctx", None),
        P(("ctx", "fsdp"), None),
        P(("ctx", "fsdp"), None),
        P(None, ("ctx", "fsdp")),
        P(("ctx", "fsdp"), None),
        P(("ctx", "fsdp"), None),
        P(("ctx", "fsdp"), None),
        P(None, ("ctx", "fsdp")),
        P(("ctx", "fsdp"), None),
        P(None, ("ctx", "fsdp")),
        P(),
        P(),
        P(),
        P(),
        P(),
        P(),
        P(),
        P(),
    )
    return jax.shard_map(
        per_device, mesh=mesh, in_specs=in_specs, out_specs=out_specs, check_vma=False
    )
```
